256 devices in a mesh: row: 64 (over x, z, core), col: 4 (over y).
Axes of the slice: x: 4, y: 4, z: 8, core: 2. Of those that a mesh axis runs over, the one named last changes fastest.
Arguments:
- cost_first: bfloat16 [8192, 102400], P('row', 'col'), may hold values from -15 to 15, as said below
- cost_second: bfloat16 [8192, 102400], P('row', 'col'), may hold values from -15 to 15, as said below
- factors: bfloat16 [102400, 128], P(('col', 'row')), may hold values from 0.25 to 4
- slab_factors: float32 [8192, 128], P('row'), may hold values from 0.25 to 4
- weights: float32 [64], replicated, may hold values from 0.5 to 2
Outputs:
- new_factors: float32 [8192, 128], P('row')
- marginal: float32 [64], replicated
The draws below stay inside these ranges and needn't reach their ends.
Inputs may be any that keep to these rules, and one draw needn't show every extreme that they name: `cost_first`: whole numbers. `cost_second`: whole numbers.
All inputs are finite; a program needn't handle non-finite values.
Results may differ from the reference program's by a relative error of at most 0.0003.
Values may be sent and summed in bfloat16 or wider, within the bound.
A program may use at most 64 MiB of HBM per device.

```python
import math
import jax
import jax.numpy as jnp
from jax import lax

N = 102400
RANK = 64
ROWS_DEV = 128
SLAB = 8192


def draw_cost_first(key, part):
    key = jax.random.fold_in(key, 11)
    hops = jax.random.randint(key, (SLAB, N), 1, 32)
    return (hops - 16).astype(jnp.float32).astype(jnp.bfloat16)


def draw_cost_second(key, part):
    key = jax.random.fold_in(key, 23)
    hops = jax.random.randint(key, (SLAB, N), 1, 32)
    return (hops - 16).astype(jnp.float32).astype(jnp.bfloat16)


def shard_levels(stream_key, shape, cuts, smallest, high):
    loudness = 1.0
    for axis_at, parts in cuts:
        draws = jax.random.uniform(jax.random.fold_in(jax.random.fold_in(stream_key, 6), axis_at), (parts,), jnp.float32, smallest / len(cuts), high / len(cuts))
        loudness = loudness * jnp.repeat(jnp.exp(draws), shape[axis_at] // parts).reshape((-1,) + (1,) * (len(shape) - 1 - axis_at))
    return loudness


def setup_inputs(seed: int = 0) -> dict:
    key_list = jax.random.split(jax.random.key(seed), 6)
    cost_first = draw_cost_first(jax.random.fold_in(key_list[5], 71), 0)
    cost_second = draw_cost_second(jax.random.fold_in(key_list[5], 71), 0)
    factors = jnp.clip(jnp.exp(math.log(4.0) - 2.7725887 * jax.random.uniform(key_list[2], (N, 2 * RANK), jnp.float32) ** shard_levels(key_list[2], (N, 2 * RANK), ((0, 256),), -0.2, 0.2)), 0.25, 4.0).astype(jnp.bfloat16)
    slab_factors = jnp.clip(jnp.exp(math.log(4.0) - 2.7725887 * jax.random.uniform(key_list[3], (SLAB, 2 * RANK), jnp.float32) ** shard_levels(key_list[3], (SLAB, 2 * RANK), ((0, 64),), -0.2, 0.2)), 0.25, 4.0)
    weights = jnp.clip(jnp.exp(jax.random.uniform(key_list[4], (RANK,), jnp.float32, math.log(0.5), math.log(2.0))), 0.5, 2.0)
    return {"cost_first": cost_first, "cost_second": cost_second, "factors": factors, "slab_factors": slab_factors, "weights": weights}


STEP = 1.0

def rank_terms(current, products, rank):
    high = lax.Precision.HIGHEST
    k_first = jnp.dot(current[:, :rank].T, products[:, :rank], precision=high)
    k_second = jnp.dot(current[:, rank:].T, products[:, rank:], precision=high)
    return jnp.concatenate([k_first, k_second], axis=1)

def normalized(current, moved):
    shifted = moved - lax.optimization_barrier(jnp.max(moved, axis=1, keepdims=True))
    tilde = current * jnp.exp(STEP * shifted)
    return tilde / lax.optimization_barrier(jnp.sum(tilde, axis=1, keepdims=True))

def advance(current, products, stats, weights, rank):
    high = lax.Precision.HIGHEST
    inverse = 1.0 / weights
    scale = 1.0 / math.sqrt(rank)
    move_first = jnp.dot(products[:, :rank] * inverse, stats[:, rank:] * inverse[None, :], precision=high) * scale
    move_second = jnp.dot(products[:, rank:] * inverse, stats[:, :rank] * inverse[None, :], precision=high) * scale
    first = normalized(current[:, :rank], move_first)
    second = normalized(current[:, rank:], move_second)
    return jnp.concatenate([first, second], axis=1)

def reference(cost_first, cost_second, factors, slab_factors, weights):
    rank = RANK
    blocks_first = cost_first.reshape(-1, ROWS_DEV, N)
    blocks_second = cost_second.reshape(-1, ROWS_DEV, N)

    def one_block(pair):
        left = jnp.dot(pair[0], factors[:, :rank], preferred_element_type=jnp.float32)
        right = jnp.dot(pair[1], factors[:, rank:], preferred_element_type=jnp.float32)
        return jnp.concatenate([left, right], axis=1)
    products = lax.map(one_block, (blocks_first, blocks_second)).reshape(SLAB, 2 * rank)
    products = products * (1.0 / (16.0 * math.sqrt(N)))
    stats = rank_terms(slab_factors, products, rank) * (1.0 / math.sqrt(SLAB))
    new_factors = advance(slab_factors, products, stats, weights, rank)
    totals = lax.optimization_barrier(jnp.sum(new_factors, axis=0))
    marginal = rank / (2.0 * SLAB) * (totals[:rank] + totals[rank:])
    return (new_factors, marginal)
```

```python
import math

import jax
import jax.numpy as jnp
from jax import lax
from jax.experimental import pallas as pl
from jax.experimental.pallas import tpu as pltpu
from jax.sharding import PartitionSpec as P

MESH = pl.DeviceIdType.MESH
HIGH = lax.Precision.HIGHEST

NX, NY, NZ = 4, 4, 8
RANK = 64
LANES = 2 * RANK
ROWS = 128
DEEP = 400
BLOCKS = 64
SLOT = 512
N = 102400
SLAB = 8192

STEPS = (
    ((1, 0), (3, 0), (0, 1), (0, 7)),
    ((1, 7), (3, 7), (3, 1), (0, 6)),
    ((1, 1), (2, 0), (0, 2), (0, 5)),
    ((2, 7), (2, 1), (3, 2), (1, 6)),
    ((1, 5), (3, 6), (0, 3), (0, 4)),
    ((2, 6), (3, 5), (3, 3), (1, 4)),
    ((2, 5), (2, 2), (1, 2), (1, 3)),
    ((2, 4), (2, 3), (3, 4), None),
)
LINKS = ((1, 0), (-1, 0), (0, 1), (0, -1))
CHUNKS = ((0, 144), (144, 128), (272, 128))


def plan():
    when = {(0, 0): -1}
    for step, row in enumerate(STEPS):
        for offset in row:
            if offset is not None:
                when[offset] = step
    queues = []
    for link, (ux, uz) in enumerate(LINKS):
        queue = []
        for step, row in enumerate(STEPS):
            if row[link] is not None:
                ox, oz = row[link]
                source = ((ox - ux) % NX, (oz - uz) % NZ)
                assert when[source] < step
                for chunk in range(len(CHUNKS)):
                    queue.append((source, when[source], step, chunk))
        queues.append(queue)
    return queues


def kernel(
    cost_first, cost_second, factors, slab, weights, new, marginal,
    costs, slots, total, turned, prods, stat, scattered, crossed, gathered, sums,
    load_sem, own_sem, send_sem, ring_sem, twin_sem,
    small_send, scatter_sem, cross_sem, gather_sem, prod_sem, sum_sem,
):
    row = lax.axis_index("row")
    y = lax.axis_index("col")
    core = lax.rem(row, 2)
    z = lax.rem(row // 2, NZ)
    x = row // (2 * NZ)
    sign = 1 - 2 * core

    def device(dx, dy, dz, dc):
        xx = lax.rem(x + dx + NX, NX)
        yy = lax.rem(y + dy + NY, NY)
        zz = lax.rem(z + dz + NZ, NZ)
        cc = lax.rem(core + dc, 2)
        return ((xx * NZ + zz) * 2 + cc, yy)

    def block(offset, way, c):
        ox, oz = offset
        ox, oz = (ox - NX if ox > NX // 2 else ox), (oz - NZ if oz > NZ // 2 else oz)
        xx = lax.rem(x - way * ox + NX, NX)
        zz = lax.rem(z - way * oz + NZ, NZ)
        return (xx * NZ + zz) * 2 + c

    def rows_of(b, start, size):
        return pl.ds(pl.multiple_of(16 * lax.rem(b, 8) + start, 16), size)

    def remote(src, dst, send, recv, to):
        return pltpu.make_async_remote_copy(
            src_ref=src, dst_ref=dst, send_sem=send, recv_sem=recv,
            device_id=to, device_id_type=MESH,
        )

    load_first = pltpu.make_async_copy(cost_first, costs.at[pl.ds(0, ROWS)], load_sem.at[0])
    load_second = pltpu.make_async_copy(cost_second, costs.at[pl.ds(ROWS, ROWS)], load_sem.at[1])
    own_slot = slots.at[row, rows_of(row, 0, DEEP)]
    load_own = pltpu.make_async_copy(factors, own_slot, own_sem)

    barrier = pltpu.get_barrier_semaphore()
    pairs = [(dy, dc) for dy in range(NY) for dc in range(2) if (dy, dc) != (0, 0)]
    greeted = [device(ux, 0, uz, 0) for ux, uz in LINKS]
    greeted += [device(0, dy, 0, dc) for dy, dc in pairs]
    for to in greeted:
        pl.semaphore_signal(barrier, inc=1, device_id=to, device_id_type=MESH)
    load_own.start()
    load_first.start()
    load_second.start()
    pl.semaphore_wait(barrier, len(greeted))

    neighbour = [device(sign * ux, 0, sign * uz, 0) for ux, uz in LINKS]
    twin = device(0, 0, 0, 1)
    queues = plan()
    heads = [0] * len(LINKS)

    def send_ready(done_step, done_chunk):
        progress = True
        while progress:
            progress = False
            for link in range(len(LINKS)):
                if heads[link] < len(queues[link]):
                    source, came, step, chunk = queues[link][heads[link]]
                    if (came, chunk) <= (done_step, done_chunk) or came < 0:
                        start, size = CHUNKS[chunk]
                        b = block(source, sign, core)
                        here = slots.at[b, rows_of(b, start, size)]
                        src = factors.at[pl.ds(start, size)] if came < 0 else here
                        remote(
                            src, here, send_sem.at[0],
                            ring_sem.at[(step * len(LINKS) + link) * len(CHUNKS) + chunk],
                            neighbour[link],
                        ).start()
                        heads[link] += 1
                        progress = True

    send_ready(-1, len(CHUNKS))
    remote(factors, own_slot, send_sem.at[0], twin_sem.at[0], twin).start()

    blank = jnp.zeros((16, LANES), jnp.bfloat16)

    def clear(group, carry):
        for m in range(8):
            for i in range(7):
                at = 16 * (i if i < m else DEEP // 16 + i)
                slots[group * 8 + m, pl.ds(at, 16), :] = blank
        return carry

    lax.fori_loop(0, BLOCKS // 8, clear, 0)
    total[...] = jnp.zeros_like(total)
    turned[...] = slab[...].T

    def multiply(blocks):
        def one(j, carry):
            b = blocks[0]
            for k in range(1, len(blocks)):
                b = jnp.where(j == k, blocks[k], b)
            at = pl.multiple_of(DEEP * b - 16 * lax.rem(b, 8), 128)
            total[...] += jnp.dot(
                costs[:, pl.ds(at, SLOT)], slots[b], preferred_element_type=jnp.float32
            )
            return carry

        lax.fori_loop(0, len(blocks), one, 0)

    def twin_wait(index, b):
        ref = slots.at[b, rows_of(b, 0, DEEP)]
        remote(ref, ref, send_sem.at[0], twin_sem.at[index], twin).wait_recv()

    mine, theirs = [((0, 0), 0)], [((0, 0), 0)]
    count = 1
    for step, offsets in enumerate(STEPS):
        arrived = []
        for chunk, (start, size) in enumerate(CHUNKS):
            for link, offset in enumerate(offsets):
                if offset is not None:
                    b = block(offset, sign, core)
                    ref = slots.at[b, rows_of(b, start, size)]
                    remote(
                        ref, ref, send_sem.at[0],
                        ring_sem.at[(step * len(LINKS) + link) * len(CHUNKS) + chunk],
                        neighbour[link],
                    ).wait_recv()
            send_ready(step, chunk)
            if chunk == len(CHUNKS) - 1:
                for offset in offsets:
                    if offset is not None:
                        b = block(offset, sign, core)
                        whole = slots.at[b, rows_of(b, 0, DEEP)]
                        remote(whole, whole, send_sem.at[0], twin_sem.at[count], twin).start()
                        arrived.append((offset, count))
                        count += 1
            if chunk == 0:
                if step == 0:
                    load_own.wait()
                    load_first.wait()
                    load_second.wait()
                multiply([block(offset, sign, core) for offset, _ in mine])
            if chunk == 1:
                for offset, index in theirs:
                    twin_wait(index, block(offset, -sign, 1 - core))
                multiply([block(offset, -sign, 1 - core) for offset, _ in theirs])
        mine = theirs = arrived
    multiply([block(offset, sign, core) for offset, _ in mine])
    for offset, index in theirs:
        twin_wait(index, block(offset, -sign, 1 - core))
    multiply([block(offset, -sign, 1 - core) for offset, _ in theirs])

    half = lax.broadcasted_iota(jnp.int32, (1, LANES), 1) < RANK
    part = jnp.where(half, total[0:ROWS, :], total[ROWS:, :]) * (1.0 / (16.0 * math.sqrt(N)))
    prods[y] = part
    terms = jnp.dot(turned[...], part, precision=HIGH, preferred_element_type=jnp.float32)
    stat[...] = jnp.where(half, terms[0:RANK, :], terms[RANK:, :])

    me = y * 2 + core
    scattered[me] = stat[pl.ds(pl.multiple_of(8 * me, 8), 8), :]
    for dy, dc in pairs:
        to = device(0, dy, 0, dc)
        g = to[1] * 2 + lax.rem(to[0], 2)
        remote(
            stat.at[pl.ds(pl.multiple_of(8 * g, 8), 8)], scattered.at[me],
            small_send.at[0], scatter_sem.at[0], to,
        ).start()
    seven = scattered.at[pl.ds(0, len(pairs))]
    pltpu.make_async_copy(seven, seven, scatter_sem.at[0]).wait()
    place = x * NZ + z
    piece = scattered[0]
    for g in range(1, 8):
        piece = piece + scattered[g]
    crossed[place] = piece
    far = [
        (dx, dz) for dz in (4, 3, 5, 2, 6, 1, 7, 0) for dx in (2, 1, 3, 0) if (dx, dz) != (0, 0)
    ]
    for dx, dz in far:
        remote(
            crossed.at[place], crossed.at[place], small_send.at[1], cross_sem.at[0],
            device(dx, 0, dz, 0),
        ).start()
    for dy in (2, 1, 3):
        remote(
            prods.at[y], prods.at[y], small_send.at[2], prod_sem.at[0], device(0, dy, 0, 0)
        ).start()
    others = crossed.at[pl.ds(0, len(far))]
    pltpu.make_async_copy(others, others, cross_sem.at[0]).wait()
    piece = jnp.sum(crossed[...], axis=0)
    mine_rows = pl.ds(pl.multiple_of(8 * me, 8), 8)
    gathered[mine_rows, :] = piece
    for dy, dc in pairs:
        remote(
            gathered.at[mine_rows], gathered.at[mine_rows], small_send.at[3], gather_sem.at[0],
            device(0, dy, 0, dc),
        ).start()
    three = prods.at[pl.ds(0, NY - 1)]
    pltpu.make_async_copy(three, three, prod_sem.at[0]).wait()
    inverse = 1.0 / weights[...]
    inverse = jnp.concatenate([inverse, inverse], axis=1)
    product = ((prods[0] + prods[1]) + prods[2]) + prods[3]
    product = product * inverse
    most = gathered.at[pl.ds(0, 8 * len(pairs))]
    pltpu.make_async_copy(most, most, gather_sem.at[0]).wait()
    stats = gathered[...] * (1.0 / math.sqrt(SLAB))
    swapped = jnp.concatenate([stats[:, RANK:], stats[:, :RANK]], axis=1) * inverse
    both = jnp.concatenate(
        [jnp.where(half, swapped, 0.0), jnp.where(half, 0.0, swapped)], axis=0
    )
    move = jnp.dot(product, both, precision=HIGH, preferred_element_type=jnp.float32)
    move = move * (1.0 / math.sqrt(RANK))
    low = jnp.max(jnp.where(half, move, -jnp.inf), axis=1, keepdims=True)
    high = jnp.max(jnp.where(half, -jnp.inf, move), axis=1, keepdims=True)
    tilde = slab[...] * jnp.exp(move - jnp.where(half, low, high))
    low = jnp.sum(jnp.where(half, tilde, 0.0), axis=1, keepdims=True)
    high = jnp.sum(jnp.where(half, 0.0, tilde), axis=1, keepdims=True)
    updated = tilde / jnp.where(half, low, high)
    sums[row] = jnp.sum(updated, axis=0, keepdims=True)
    for dx, dz in far + [(0, 0)]:
        for dc in (0, 1):
            if (dx, dz, dc) != (0, 0, 0):
                remote(
                    sums.at[row], sums.at[row], small_send.at[4], sum_sem.at[0],
                    device(dx, 0, dz, dc),
                ).start()
    new[...] = updated

    rest = sums.at[pl.ds(0, BLOCKS - 1)]
    sent = slots.at[pl.ds(0, BLOCKS - 1), pl.ds(0, DEEP)]
    pltpu.make_async_copy(sent, sent, send_sem.at[0]).wait()
    pltpu.make_async_copy(seven, seven, small_send.at[0]).wait()
    pltpu.make_async_copy(others, others, small_send.at[1]).wait()
    pltpu.make_async_copy(three, three, small_send.at[2]).wait()
    pltpu.make_async_copy(most, most, small_send.at[3]).wait()
    pltpu.make_async_copy(rest, rest, sum_sem.at[0]).wait()
    sums_all = jnp.sum(sums[...], axis=0)
    marginal[...] = (RANK / (2.0 * SLAB)) * (sums_all[:, :RANK] + sums_all[:, RANK:])
    pltpu.make_async_copy(rest, rest, small_send.at[4]).wait()


def local(cost_first, cost_second, factors, slab_factors, weights):
    vmem = pl.BlockSpec(memory_space=pltpu.VMEM)
    hbm = pl.BlockSpec(memory_space=pl.ANY)
    f32 = jnp.float32
    dma = pltpu.SemaphoreType.DMA
    new, marginal = pl.pallas_call(
        kernel,
        out_shape=(
            jax.ShapeDtypeStruct((ROWS, LANES), f32),
            jax.ShapeDtypeStruct((1, RANK), f32),
        ),
        in_specs=[hbm, hbm, hbm, vmem, vmem],
        out_specs=(vmem, vmem),
        scratch_shapes=[
            pltpu.VMEM((2 * ROWS, BLOCKS * DEEP), jnp.bfloat16),
            pltpu.VMEM((BLOCKS, SLOT, LANES), jnp.bfloat16),
            pltpu.VMEM((2 * ROWS, LANES), f32),
            pltpu.VMEM((LANES, ROWS), f32),
            pltpu.VMEM((NY, ROWS, LANES), f32),
            pltpu.VMEM((RANK, LANES), f32),
            pltpu.VMEM((8, 8, LANES), f32),
            pltpu.VMEM((NX * NZ, 8, LANES), f32),
            pltpu.VMEM((RANK, LANES), f32),
            pltpu.VMEM((BLOCKS, 1, LANES), f32),
            dma((2,)),
            dma,
            dma((1,)),
            dma((len(STEPS) * len(LINKS) * len(CHUNKS),)),
            dma((NX * NZ,)),
            dma((5,)),
            dma((1,)),
            dma((1,)),
            dma((1,)),
            dma((1,)),
            dma((1,)),
        ],
        compiler_params=pltpu.CompilerParams(
            collective_id=0, has_side_effects=True, vmem_limit_bytes=44 << 20
        ),
    )(cost_first, cost_second, factors, slab_factors, weights.reshape(1, RANK))
    return new, marginal.reshape(RANK)


def solution(mesh):
    placed = (P("row", "col"), P("row", "col"), P(("col", "row"), None), P("row", None), P())
    return jax.shard_map(
        local, mesh=mesh, in_specs=placed, out_specs=(P("row", None), P()), check_vma=False
    )
```

```python
import math

import jax
import jax.numpy as jnp
from jax import lax
from jax.experimental import pallas as pl
from jax.experimental.pallas import tpu as pltpu
from jax.sharding import PartitionSpec as P

MESH = pl.DeviceIdType.MESH
HIGH = lax.Precision.HIGHEST

NX, NY, NZ = 4, 4, 8
RANK = 64
LANES = 2 * RANK
ROWS = 128
DEEP = 400
BLOCKS = 64
SLOT = 512
N = 102400
SLAB = 8192

STEPS = (
    ((1, 0), (3, 0), (0, 1), (0, 7)),
    ((1, 7), (3, 7), (3, 1), (0, 6)),
    ((1, 1), (2, 0), (0, 2), (0, 5)),
    ((2, 7), (2, 1), (3, 2), (1, 6)),
    ((1, 5), (3, 6), (0, 3), (0, 4)),
    ((2, 6), (3, 5), (3, 3), (1, 4)),
    ((2, 5), (2, 2), (1, 2), (1, 3)),
    ((2, 4), (2, 3), (3, 4), None),
)
LINKS = ((1, 0), (-1, 0), (0, 1), (0, -1))
CHUNKS = ((0, 144), (144, 128), (272, 128))


def plan():
    when = {(0, 0): -1}
    for step, row in enumerate(STEPS):
        for offset in row:
            if offset is not None:
                when[offset] = step
    queues = []
    for link, (ux, uz) in enumerate(LINKS):
        queue = []
        for step, row in enumerate(STEPS):
            if row[link] is not None:
                ox, oz = row[link]
                source = ((ox - ux) % NX, (oz - uz) % NZ)
                assert when[source] < step
                for chunk in range(len(CHUNKS)):
                    queue.append((source, when[source], step, chunk))
        queues.append(queue)
    return queues


def kernel(
    cost_first, cost_second, factors, slab_in, weights_in, new, marginal,
    slab, twin_slab, weights, costs, twins, slots, total, turned, halves, outgoing, prods,
    stat, scattered, crossed, gathered, sums,
    load_sem, own_sem, send_sem, ring_sem, twin_sem, slab_sem, half_sem,
    small_send, scatter_sem, cross_sem, gather_sem, prod_sem, sum_sem,
):
    row = lax.axis_index("row")
    y = lax.axis_index("col")
    core = lax.rem(row, 2)
    z = lax.rem(row // 2, NZ)
    x = row // (2 * NZ)
    sign = 1 - 2 * core

    def device(dx, dy, dz, dc):
        xx = lax.rem(x + dx + NX, NX)
        yy = lax.rem(y + dy + NY, NY)
        zz = lax.rem(z + dz + NZ, NZ)
        cc = lax.rem(core + dc, 2)
        return ((xx * NZ + zz) * 2 + cc, yy)

    def block(offset, way, c):
        ox, oz = offset
        ox, oz = (ox - NX if ox > NX // 2 else ox), (oz - NZ if oz > NZ // 2 else oz)
        xx = lax.rem(x - way * ox + NX, NX)
        zz = lax.rem(z - way * oz + NZ, NZ)
        return (xx * NZ + zz) * 2 + c

    def rows_of(b, start, size):
        return pl.ds(pl.multiple_of(16 * lax.rem(b, 8) + start, 16), size)

    def column(b):
        return pl.multiple_of(DEEP * b - 16 * lax.rem(b, 8), 128)

    def remote(src, dst, send, recv, to):
        return pltpu.make_async_remote_copy(
            src_ref=src, dst_ref=dst, send_sem=send, recv_sem=recv,
            device_id=to, device_id_type=MESH,
        )

    load_first = pltpu.make_async_copy(cost_first, costs.at[pl.ds(0, ROWS)], load_sem.at[0])
    load_second = pltpu.make_async_copy(cost_second, costs.at[pl.ds(ROWS, ROWS)], load_sem.at[1])
    place = x * NZ + z
    own_slot = slots.at[place, rows_of(row, 0, DEEP)]
    load_own = pltpu.make_async_copy(factors, own_slot, own_sem)
    load_slab = pltpu.make_async_copy(slab_in, slab, load_sem.at[2])
    load_weights = pltpu.make_async_copy(weights_in, weights, load_sem.at[3])

    barrier = pltpu.get_barrier_semaphore()
    pairs = [(dy, dc) for dy in range(NY) for dc in range(2) if (dy, dc) != (0, 0)]
    greeted = [device(ux, 0, uz, 0) for ux, uz in LINKS]
    greeted += [device(0, dy, 0, dc) for dy, dc in pairs]
    for to in greeted:
        pl.semaphore_signal(barrier, inc=1, device_id=to, device_id_type=MESH)
    load_slab.start()
    load_weights.start()
    load_own.start()
    load_first.start()
    load_second.start()
    pl.semaphore_wait(barrier, len(greeted))

    neighbour = [device(sign * ux, 0, sign * uz, 0) for ux, uz in LINKS]
    twin = device(0, 0, 0, 1)
    queues = plan()
    heads = [0] * len(LINKS)

    def send_ready(done_step, done_chunk):
        progress = True
        while progress:
            progress = False
            for link in range(len(LINKS)):
                if heads[link] < len(queues[link]):
                    source, came, step, chunk = queues[link][heads[link]]
                    if (came, chunk) <= (done_step, done_chunk) or came < 0:
                        start, size = CHUNKS[chunk]
                        b = block(source, sign, core)
                        here = slots.at[b // 2, rows_of(b, start, size)]
                        src = factors.at[pl.ds(start, size)] if came < 0 else here
                        remote(
                            src, here, send_sem.at[0],
                            ring_sem.at[(step * len(LINKS) + link) * len(CHUNKS) + chunk],
                            neighbour[link],
                        ).start()
                        heads[link] += 1
                        progress = True

    send_ready(-1, len(CHUNKS))

    order = [(0, 0)] + [offset for row_of in STEPS for offset in row_of if offset is not None]

    def lend(indices):
        for k in indices:
            if k < len(order):
                b = block(order[k], -sign, 1 - core)
                at = pl.ds(column(b), SLOT)
                for part, cost in enumerate((cost_first, cost_second)):
                    remote(
                        cost.at[:, at], twins.at[k, pl.ds(part * ROWS, ROWS)],
                        send_sem.at[1], twin_sem.at[k], twin,
                    ).start()

    lend(range(0, 9))
    remote(slab_in, twin_slab, send_sem.at[2], slab_sem, twin).start()

    blank = jnp.zeros((16, LANES), jnp.bfloat16)

    def clear(group, carry):
        for j in range(4):
            m = 2 * j + core
            for i in range(7):
                at = pl.multiple_of(16 * (i + jnp.where(i < m, 0, DEEP // 16)), 16)
                slots[group * 4 + j, pl.ds(at, 16), :] = blank
        return carry

    lax.fori_loop(0, NX * NZ // 4, clear, 0)
    total[...] = jnp.zeros_like(total)
    load_slab.wait()
    load_weights.wait()
    turned[:, 0:ROWS] = slab[...].T

    def multiply(first, offsets):
        blocks = [block(offset, sign, core) for offset in offsets]
        for k in range(len(blocks)):
            ref = twins.at[first + k]
            pltpu.make_async_copy(ref, ref, twin_sem.at[first + k]).wait()

        def one(j, carry):
            b = blocks[0]
            for k in range(1, len(blocks)):
                b = jnp.where(j == k, blocks[k], b)
            left = jnp.concatenate([costs[:, pl.ds(column(b), SLOT)], twins[first + j]], axis=0)
            total[...] += jnp.dot(left, slots[b // 2], preferred_element_type=jnp.float32)
            return carry

        lax.fori_loop(0, len(blocks), one, 0)

    ready, first = [(0, 0)], 0
    for step, offsets in enumerate(STEPS):
        for chunk, (start, size) in enumerate(CHUNKS):
            for link, offset in enumerate(offsets):
                if offset is not None:
                    b = block(offset, sign, core)
                    ref = slots.at[b // 2, rows_of(b, start, size)]
                    remote(
                        ref, ref, send_sem.at[0],
                        ring_sem.at[(step * len(LINKS) + link) * len(CHUNKS) + chunk],
                        neighbour[link],
                    ).wait_recv()
            send_ready(step, chunk)
            if chunk == 0:
                lend(range(4 * step + 9, 4 * step + 13))
                if step == 0:
                    load_own.wait()
                    load_first.wait()
                    load_second.wait()
                multiply(first, ready)
                first += len(ready)
        ready = [offset for offset in offsets if offset is not None]
    multiply(first, ready)

    half = lax.broadcasted_iota(jnp.int32, (1, LANES), 1) < RANK
    scale = 1.0 / (16.0 * math.sqrt(N))
    part = jnp.where(half, total[0:ROWS, :], total[ROWS : 2 * ROWS, :]) * scale
    lent = jnp.where(half, total[2 * ROWS : 3 * ROWS, :], total[3 * ROWS :, :]) * scale
    outgoing[...] = lent
    hand = remote(outgoing, halves.at[core], small_send.at[5], half_sem, twin)
    hand.start()
    halves[core] = part
    remote(slab_in, twin_slab, send_sem.at[2], slab_sem, twin).wait_recv()
    turned[:, ROWS:] = twin_slab[...].T
    terms = jnp.dot(
        turned[...], jnp.concatenate([part, lent], axis=0), precision=HIGH,
        preferred_element_type=jnp.float32,
    )
    stat[...] = jnp.where(half, terms[0:RANK, :], terms[RANK:, :])

    me = y * 2 + core
    scattered[me] = stat[pl.ds(pl.multiple_of(8 * me, 8), 8), :]
    for dy, dc in pairs:
        to = device(0, dy, 0, dc)
        g = to[1] * 2 + lax.rem(to[0], 2)
        remote(
            stat.at[pl.ds(pl.multiple_of(8 * g, 8), 8)], scattered.at[me],
            small_send.at[0], scatter_sem.at[0], to,
        ).start()
    hand.wait()
    prods[y] = halves[0] + halves[1]
    for dy in (2, 1, 3):
        remote(
            prods.at[y], prods.at[y], small_send.at[2], prod_sem.at[0], device(0, dy, 0, 0)
        ).start()
    seven = scattered.at[pl.ds(0, len(pairs))]
    pltpu.make_async_copy(seven, seven, scatter_sem.at[0]).wait()
    piece = scattered[0]
    for g in range(1, 8):
        piece = piece + scattered[g]
    crossed[place] = piece
    far = [
        (dx, dz) for dz in (4, 3, 5, 2, 6, 1, 7, 0) for dx in (2, 1, 3, 0) if (dx, dz) != (0, 0)
    ]
    for dx, dz in far:
        remote(
            crossed.at[place], crossed.at[place], small_send.at[1], cross_sem.at[0],
            device(dx, 0, dz, 0),
        ).start()
    others = crossed.at[pl.ds(0, len(far))]
    pltpu.make_async_copy(others, others, cross_sem.at[0]).wait()
    piece = jnp.sum(crossed[...], axis=0)
    mine_rows = pl.ds(pl.multiple_of(8 * me, 8), 8)
    gathered[mine_rows, :] = piece
    for dy, dc in pairs:
        remote(
            gathered.at[mine_rows], gathered.at[mine_rows], small_send.at[3], gather_sem.at[0],
            device(0, dy, 0, dc),
        ).start()
    three = prods.at[pl.ds(0, NY - 1)]
    pltpu.make_async_copy(three, three, prod_sem.at[0]).wait()
    inverse = 1.0 / weights[...]
    inverse = jnp.concatenate([inverse, inverse], axis=1)
    product = ((prods[0] + prods[1]) + prods[2]) + prods[3]
    product = product * inverse
    most = gathered.at[pl.ds(0, 8 * len(pairs))]
    pltpu.make_async_copy(most, most, gather_sem.at[0]).wait()
    stats = gathered[...] * (1.0 / math.sqrt(SLAB))
    swapped = jnp.concatenate([stats[:, RANK:], stats[:, :RANK]], axis=1) * inverse
    both = jnp.concatenate(
        [jnp.where(half, swapped, 0.0), jnp.where(half, 0.0, swapped)], axis=0
    )
    move = jnp.dot(product, both, precision=HIGH, preferred_element_type=jnp.float32)
    move = move * (1.0 / math.sqrt(RANK))
    low = jnp.max(jnp.where(half, move, -jnp.inf), axis=1, keepdims=True)
    high = jnp.max(jnp.where(half, -jnp.inf, move), axis=1, keepdims=True)
    tilde = slab[...] * jnp.exp(move - jnp.where(half, low, high))
    low = jnp.sum(jnp.where(half, tilde, 0.0), axis=1, keepdims=True)
    high = jnp.sum(jnp.where(half, 0.0, tilde), axis=1, keepdims=True)
    result = tilde / jnp.where(half, low, high)
    sums[row] = jnp.sum(result, axis=0, keepdims=True)
    for dx, dz in far + [(0, 0)]:
        for dc in (0, 1):
            if (dx, dz, dc) != (0, 0, 0):
                remote(
                    sums.at[row], sums.at[row], small_send.at[4], sum_sem.at[0],
                    device(dx, 0, dz, dc),
                ).start()
    new[...] = result

    rest = sums.at[pl.ds(0, BLOCKS - 1)]
    sent = slots.at[pl.ds(0, NX * NZ - 1), pl.ds(0, DEEP)]
    pltpu.make_async_copy(sent, sent, send_sem.at[0]).wait()
    pltpu.make_async_copy(twins, twins, send_sem.at[1]).wait()
    remote(slab_in, twin_slab, send_sem.at[2], slab_sem, twin).wait_send()
    pltpu.make_async_copy(seven, seven, small_send.at[0]).wait()
    pltpu.make_async_copy(others, others, small_send.at[1]).wait()
    pltpu.make_async_copy(three, three, small_send.at[2]).wait()
    pltpu.make_async_copy(most, most, small_send.at[3]).wait()
    pltpu.make_async_copy(rest, rest, sum_sem.at[0]).wait()
    sums_all = jnp.sum(sums[...], axis=0)
    marginal[...] = (RANK / (2.0 * SLAB)) * (sums_all[:, :RANK] + sums_all[:, RANK:])
    pltpu.make_async_copy(rest, rest, small_send.at[4]).wait()


def finish(new_in, marginal_in, new, marginal, sems):
    first = pltpu.make_async_copy(new_in, new, sems.at[0])
    second = pltpu.make_async_copy(marginal_in, marginal, sems.at[1])
    first.start()
    second.start()
    first.wait()
    second.wait()


def local(cost_first, cost_second, factors, slab_factors, weights):
    hbm = pl.BlockSpec(memory_space=pltpu.HBM)
    vmem = pl.BlockSpec(memory_space=pltpu.VMEM)
    f32, bf16 = jnp.float32, jnp.bfloat16
    dma = pltpu.SemaphoreType.DMA
    shapes = (
        jax.ShapeDtypeStruct((ROWS, LANES), f32),
        jax.ShapeDtypeStruct((1, RANK), f32),
    )
    new, marginal = pl.pallas_call(
        kernel,
        out_shape=tuple(pltpu.VMEM(shape.shape, shape.dtype) for shape in shapes),
        in_specs=[hbm] * 5,
        out_specs=(vmem, vmem),
        scratch_shapes=[
            pltpu.VMEM((ROWS, LANES), f32),
            pltpu.VMEM((ROWS, LANES), f32),
            pltpu.VMEM((1, RANK), f32),
            pltpu.VMEM((2 * ROWS, BLOCKS * DEEP), bf16),
            pltpu.VMEM((NX * NZ, 2 * ROWS, SLOT), bf16),
            pltpu.VMEM((NX * NZ, SLOT, LANES), bf16),
            pltpu.VMEM((4 * ROWS, LANES), f32),
            pltpu.VMEM((LANES, 2 * ROWS), f32),
            pltpu.VMEM((2, ROWS, LANES), f32),
            pltpu.VMEM((ROWS, LANES), f32),
            pltpu.VMEM((NY, ROWS, LANES), f32),
            pltpu.VMEM((RANK, LANES), f32),
            pltpu.VMEM((8, 8, LANES), f32),
            pltpu.VMEM((NX * NZ, 8, LANES), f32),
            pltpu.VMEM((RANK, LANES), f32),
            pltpu.VMEM((BLOCKS, 1, LANES), f32),
            dma((4,)),
            dma,
            dma((3,)),
            dma((len(STEPS) * len(LINKS) * len(CHUNKS),)),
            dma((NX * NZ,)),
            dma,
            dma,
            dma((6,)),
            dma((1,)),
            dma((1,)),
            dma((1,)),
            dma((1,)),
            dma((1,)),
        ],
        compiler_params=pltpu.CompilerParams(
            collective_id=0, has_side_effects=True, vmem_limit_bytes=60 << 20
        ),
    )(cost_first, cost_second, factors, slab_factors, weights.reshape(1, RANK))
    new, marginal = pl.pallas_call(
        finish,
        out_shape=shapes,
        in_specs=[vmem] * 2,
        out_specs=(hbm, hbm),
        scratch_shapes=[dma((2,))],
        compiler_params=pltpu.CompilerParams(vmem_limit_bytes=1 << 20),
    )(new, marginal)
    return new, marginal.reshape(RANK)


def solution(mesh):
    placed = (P("row", "col"), P("row", "col"), P(("col", "row"), None), P("row", None), P())
    return jax.shard_map(
        local, mesh=mesh, in_specs=placed, out_specs=(P("row", None), P()), check_vma=False
    )
```

```python
import math

import jax
import jax.numpy as jnp
from jax import lax
from jax.experimental import pallas as pl
from jax.experimental.pallas import tpu as pltpu
from jax.sharding import PartitionSpec as P

MESH = pl.DeviceIdType.MESH
HIGH = lax.Precision.HIGHEST

NX, NY, NZ = 4, 4, 8
RANK = 64
LANES = 2 * RANK
ROWS = 128
DEEP = 400
BLOCKS = 64
SLOT = 512
N = 102400
SLAB = 8192

AHEAD = 9
LINKS = ((1, 0), (-1, 0), (0, 1), (0, -1))
CHUNKS = ((0, 144), (144, 128), (272, 128))
SENT = (
    (
        64, 65, 66, 120, 128, 121, 129, 130, 112, 113, 184, 114, 185, 144, 145, 146,
        176, 178, 153, 154, 170,
    ),
    (
        192, 193, 194, 200, 201, 202, 248, 250, 136, 137, 138, 208, 186, 232, 233, 18,
        234, 177, 168, 169, 24, 25, 26, 161,
    ),
    (
        8, 9, 10, 72, 73, 74, 16, 17, 80, 81, 82, 209, 210, 88, 89, 90,
        216, 217, 152, 218, 96, 98, 160, 162,
    ),
    (
        56, 57, 58, 48, 49, 50, 249, 122, 40, 41, 42, 240, 241, 242, 104, 105,
        106, 32, 224, 225, 97, 226, 33, 34,
    ),
)
TURNS = (
    64, 192, 8, 56, -1, 65, 193, 9, 57, 66, 194, 10, 58, -9, -25, -2,
    -8, 72, 200, 120, 48, 73, 201, 49, 128, 74, 202, 121, 50, -10, 16, 248,
    129, 249, -26, 17, -7, 250, 130, 122, -32, 80, 136, 112, 40, -17, 81, 137,
    113, 41, -16, 82, 138, 42, 184, -11, 209, -18, 208, 114, 240, 210, -6, 186,
    185, 241, -15, 88, -27, 232, 242, 144, 89, -24, 233, 145, 104, 90, 18, 146,
    105, -31, -12, 216, 234, 106, 176, -3, 217, 177, 178, 32, -19, -30, 168, 224,
    152, 153, -14, 169, 225, 218, 154, -23, 24, 97, 96, -28, -20, 25, 170, 226,
    98, -22, -29, 26, 33, -13, -4, 34, 160, -5, 161, 162, -21,
)


def kernel(
    cost_first, cost_second, factors, slab_in, weights_in, new, marginal,
    slab, twin_slab, weights, costs, twins, slots, total, turned, halves, outgoing, prods,
    stat, scattered, crossed, gathered, sums,
    load_sem, own_sem, send_sem, ring_sem, twin_sem, slab_sem, half_sem,
    small_send, scatter_sem, cross_sem, gather_sem, prod_sem, sum_sem,
):
    row = lax.axis_index("row")
    y = lax.axis_index("col")
    core = lax.rem(row, 2)
    z = lax.rem(row // 2, NZ)
    x = row // (2 * NZ)
    sign = 1 - 2 * core

    def device(dx, dy, dz, dc):
        xx = lax.rem(x + dx + NX, NX)
        yy = lax.rem(y + dy + NY, NY)
        zz = lax.rem(z + dz + NZ, NZ)
        cc = lax.rem(core + dc, 2)
        return ((xx * NZ + zz) * 2 + cc, yy)

    def block(offset, way, c):
        ox, oz = offset
        ox, oz = (ox - NX if ox > NX // 2 else ox), (oz - NZ if oz > NZ // 2 else oz)
        xx = lax.rem(x - way * ox + NX, NX)
        zz = lax.rem(z - way * oz + NZ, NZ)
        return (xx * NZ + zz) * 2 + c

    def rows_of(b, start, size):
        return pl.ds(pl.multiple_of(16 * lax.rem(b, 8) + start, 16), size)

    def column(b):
        return pl.multiple_of(DEEP * b - 16 * lax.rem(b, 8), 128)

    def remote(src, dst, send, recv, to):
        return pltpu.make_async_remote_copy(
            src_ref=src, dst_ref=dst, send_sem=send, recv_sem=recv,
            device_id=to, device_id_type=MESH,
        )

    load_first = pltpu.make_async_copy(cost_first, costs.at[pl.ds(0, ROWS)], load_sem.at[0])
    load_second = pltpu.make_async_copy(cost_second, costs.at[pl.ds(ROWS, ROWS)], load_sem.at[1])
    place = x * NZ + z
    own_slot = slots.at[place, rows_of(row, 0, DEEP)]
    load_own = pltpu.make_async_copy(factors, own_slot, own_sem)
    load_slab = pltpu.make_async_copy(slab_in, slab, load_sem.at[2])
    load_weights = pltpu.make_async_copy(weights_in, weights, load_sem.at[3])

    barrier = pltpu.get_barrier_semaphore()
    pairs = [(dy, dc) for dy in range(NY) for dc in range(2) if (dy, dc) != (0, 0)]
    greeted = [device(ux, 0, uz, 0) for ux, uz in LINKS]
    greeted += [device(0, dy, 0, dc) for dy, dc in pairs]
    for to in greeted:
        pl.semaphore_signal(barrier, inc=1, device_id=to, device_id_type=MESH)
    load_slab.start()
    load_weights.start()
    load_own.start()
    load_first.start()
    load_second.start()
    pl.semaphore_wait(barrier, len(greeted))

    neighbour = [device(sign * ux, 0, sign * uz, 0) for ux, uz in LINKS]
    twin = device(0, 0, 0, 1)
    heads = [0] * len(LINKS)
    here = {chunk for chunk in range(len(CHUNKS))}

    def spot(offset, chunk):
        start, size = CHUNKS[chunk]
        b = block(offset, sign, core)
        return slots.at[b // 2, rows_of(b, start, size)]

    def send_ready():
        progress = True
        while progress:
            progress = False
            for link, (ux, uz) in enumerate(LINKS):
                if heads[link] < len(SENT[link]):
                    code = SENT[link][heads[link]]
                    dx, dz, chunk = code // 64, code // 8 % 8, code % 8
                    dx, dz = (dx - ux) % NX, (dz - uz) % NZ
                    if 64 * dx + 8 * dz + chunk in here:
                        dst = spot((dx, dz), chunk)
                        src = factors.at[pl.ds(*CHUNKS[chunk])] if dx == dz == 0 else dst
                        remote(
                            src, dst, send_sem.at[0], ring_sem.at[code], neighbour[link]
                        ).start()
                        heads[link] += 1
                        progress = True

    send_ready()

    order = [((-1 - turn) // 8, (-1 - turn) % 8) for turn in TURNS if turn < 0]

    def lend(indices):
        for k in indices:
            if k < len(order):
                b = block(order[k], -sign, 1 - core)
                at = pl.ds(column(b), SLOT)
                for part, cost in enumerate((cost_first, cost_second)):
                    remote(
                        cost.at[:, at], twins.at[k, pl.ds(part * ROWS, ROWS)],
                        send_sem.at[1], twin_sem.at[k], twin,
                    ).start()

    lend(range(AHEAD))
    remote(slab_in, twin_slab, send_sem.at[2], slab_sem, twin).start()

    blank = jnp.zeros((16, LANES), jnp.bfloat16)

    def clear(group, carry):
        for j in range(4):
            m = 2 * j + core
            for i in range(7):
                at = pl.multiple_of(16 * (i + jnp.where(i < m, 0, DEEP // 16)), 16)
                slots[group * 4 + j, pl.ds(at, 16), :] = blank
        return carry

    lax.fori_loop(0, NX * NZ // 4, clear, 0)
    total[...] = jnp.zeros_like(total)
    load_slab.wait()
    load_weights.wait()
    turned[:, 0:ROWS] = slab[...].T

    def multiply(k):
        lend(range(k + AHEAD, k + AHEAD + 1))
        if k == 0:
            load_own.wait()
            load_first.wait()
            load_second.wait()
        b = block(order[k], sign, core)
        ref = twins.at[k]
        pltpu.make_async_copy(ref, ref, twin_sem.at[k]).wait()
        left = jnp.concatenate([costs[:, pl.ds(column(b), SLOT)], ref[...]], axis=0)
        total[...] += jnp.dot(left, slots[b // 2], preferred_element_type=jnp.float32)

    done = 0
    for turn in TURNS:
        if turn < 0:
            multiply(done)
            done += 1
        else:
            chunk = spot((turn // 64, turn // 8 % 8), turn % 8)
            remote(chunk, chunk, send_sem.at[0], ring_sem.at[turn], neighbour[0]).wait_recv()
            here.add(turn)
            send_ready()

    half = lax.broadcasted_iota(jnp.int32, (1, LANES), 1) < RANK
    scale = 1.0 / (16.0 * math.sqrt(N))
    part = jnp.where(half, total[0:ROWS, :], total[ROWS : 2 * ROWS, :]) * scale
    lent = jnp.where(half, total[2 * ROWS : 3 * ROWS, :], total[3 * ROWS :, :]) * scale
    outgoing[...] = lent
    hand = remote(outgoing, halves.at[core], small_send.at[5], half_sem, twin)
    hand.start()
    halves[core] = part
    remote(slab_in, twin_slab, send_sem.at[2], slab_sem, twin).wait_recv()
    turned[:, ROWS:] = twin_slab[...].T
    terms = jnp.dot(
        turned[...], jnp.concatenate([part, lent], axis=0), precision=HIGH,
        preferred_element_type=jnp.float32,
    )
    stat[...] = jnp.where(half, terms[0:RANK, :], terms[RANK:, :])

    me = y * 2 + core
    scattered[me] = stat[pl.ds(pl.multiple_of(8 * me, 8), 8), :]
    for dy, dc in pairs:
        to = device(0, dy, 0, dc)
        g = to[1] * 2 + lax.rem(to[0], 2)
        remote(
            stat.at[pl.ds(pl.multiple_of(8 * g, 8), 8)], scattered.at[me],
            small_send.at[0], scatter_sem.at[0], to,
        ).start()
    seven = scattered.at[pl.ds(0, len(pairs))]
    pltpu.make_async_copy(seven, seven, scatter_sem.at[0]).wait()
    piece = scattered[0]
    for g in range(1, 8):
        piece = piece + scattered[g]
    crossed[place] = piece
    far = [
        (dx, dz) for dz in (4, 3, 5, 2, 6, 1, 7, 0) for dx in (2, 1, 3, 0) if (dx, dz) != (0, 0)
    ]
    for dx, dz in far:
        remote(
            crossed.at[place], crossed.at[place], small_send.at[1], cross_sem.at[0],
            device(dx, 0, dz, 0),
        ).start()
    hand.wait()
    prods[y] = halves[0] + halves[1]
    for dy in (2, 1, 3):
        remote(
            prods.at[y], prods.at[y], small_send.at[2], prod_sem.at[0], device(0, dy, 0, 0)
        ).start()
    others = crossed.at[pl.ds(0, len(far))]
    pltpu.make_async_copy(others, others, cross_sem.at[0]).wait()
    piece = jnp.sum(crossed[...], axis=0)
    mine_rows = pl.ds(pl.multiple_of(8 * me, 8), 8)
    gathered[mine_rows, :] = piece
    for dy, dc in pairs:
        remote(
            gathered.at[mine_rows], gathered.at[mine_rows], small_send.at[3], gather_sem.at[0],
            device(0, dy, 0, dc),
        ).start()
    three = prods.at[pl.ds(0, NY - 1)]
    pltpu.make_async_copy(three, three, prod_sem.at[0]).wait()
    inverse = 1.0 / weights[...]
    inverse = jnp.concatenate([inverse, inverse], axis=1)
    product = ((prods[0] + prods[1]) + prods[2]) + prods[3]
    product = product * inverse
    most = gathered.at[pl.ds(0, 8 * len(pairs))]
    pltpu.make_async_copy(most, most, gather_sem.at[0]).wait()
    stats = gathered[...] * (1.0 / math.sqrt(SLAB))
    swapped = jnp.concatenate([stats[:, RANK:], stats[:, :RANK]], axis=1) * inverse
    both = jnp.concatenate(
        [jnp.where(half, swapped, 0.0), jnp.where(half, 0.0, swapped)], axis=0
    )
    move = jnp.dot(product, both, precision=HIGH, preferred_element_type=jnp.float32)
    move = move * (1.0 / math.sqrt(RANK))
    low = jnp.max(jnp.where(half, move, -jnp.inf), axis=1, keepdims=True)
    high = jnp.max(jnp.where(half, -jnp.inf, move), axis=1, keepdims=True)
    tilde = slab[...] * jnp.exp(move - jnp.where(half, low, high))
    low = jnp.sum(jnp.where(half, tilde, 0.0), axis=1, keepdims=True)
    high = jnp.sum(jnp.where(half, 0.0, tilde), axis=1, keepdims=True)
    result = tilde / jnp.where(half, low, high)
    sums[row] = jnp.sum(result, axis=0, keepdims=True)
    for dx, dz in far + [(0, 0)]:
        for dc in (0, 1):
            if (dx, dz, dc) != (0, 0, 0):
                remote(
                    sums.at[row], sums.at[row], small_send.at[4], sum_sem.at[0],
                    device(dx, 0, dz, dc),
                ).start()
    new[...] = result

    rest = sums.at[pl.ds(0, BLOCKS - 1)]
    sent = slots.at[pl.ds(0, NX * NZ - 1), pl.ds(0, DEEP)]
    pltpu.make_async_copy(sent, sent, send_sem.at[0]).wait()
    pltpu.make_async_copy(twins, twins, send_sem.at[1]).wait()
    remote(slab_in, twin_slab, send_sem.at[2], slab_sem, twin).wait_send()
    pltpu.make_async_copy(seven, seven, small_send.at[0]).wait()
    pltpu.make_async_copy(others, others, small_send.at[1]).wait()
    pltpu.make_async_copy(three, three, small_send.at[2]).wait()
    pltpu.make_async_copy(most, most, small_send.at[3]).wait()
    pltpu.make_async_copy(rest, rest, sum_sem.at[0]).wait()
    sums_all = jnp.sum(sums[...], axis=0)
    marginal[...] = (RANK / (2.0 * SLAB)) * (sums_all[:, :RANK] + sums_all[:, RANK:])
    pltpu.make_async_copy(rest, rest, small_send.at[4]).wait()


def finish(new_in, marginal_in, new, marginal, sems):
    first = pltpu.make_async_copy(new_in, new, sems.at[0])
    second = pltpu.make_async_copy(marginal_in, marginal, sems.at[1])
    first.start()
    second.start()
    first.wait()
    second.wait()


def local(cost_first, cost_second, factors, slab_factors, weights):
    hbm = pl.BlockSpec(memory_space=pltpu.HBM)
    vmem = pl.BlockSpec(memory_space=pltpu.VMEM)
    f32, bf16 = jnp.float32, jnp.bfloat16
    dma = pltpu.SemaphoreType.DMA
    shapes = (
        jax.ShapeDtypeStruct((ROWS, LANES), f32),
        jax.ShapeDtypeStruct((1, RANK), f32),
    )
    new, marginal = pl.pallas_call(
        kernel,
        out_shape=tuple(pltpu.VMEM(shape.shape, shape.dtype) for shape in shapes),
        in_specs=[hbm] * 5,
        out_specs=(vmem, vmem),
        scratch_shapes=[
            pltpu.VMEM((ROWS, LANES), f32),
            pltpu.VMEM((ROWS, LANES), f32),
            pltpu.VMEM((1, RANK), f32),
            pltpu.VMEM((2 * ROWS, BLOCKS * DEEP), bf16),
            pltpu.VMEM((NX * NZ, 2 * ROWS, SLOT), bf16),
            pltpu.VMEM((NX * NZ, SLOT, LANES), bf16),
            pltpu.VMEM((4 * ROWS, LANES), f32),
            pltpu.VMEM((LANES, 2 * ROWS), f32),
            pltpu.VMEM((2, ROWS, LANES), f32),
            pltpu.VMEM((ROWS, LANES), f32),
            pltpu.VMEM((NY, ROWS, LANES), f32),
            pltpu.VMEM((RANK, LANES), f32),
            pltpu.VMEM((8, 8, LANES), f32),
            pltpu.VMEM((NX * NZ, 8, LANES), f32),
            pltpu.VMEM((RANK, LANES), f32),
            pltpu.VMEM((BLOCKS, 1, LANES), f32),
            dma((4,)),
            dma,
            dma((3,)),
            dma((8 * NX * NZ,)),
            dma((NX * NZ,)),
            dma,
            dma,
            dma((6,)),
            dma((1,)),
            dma((1,)),
            dma((1,)),
            dma((1,)),
            dma((1,)),
        ],
        compiler_params=pltpu.CompilerParams(
            collective_id=0, has_side_effects=True, vmem_limit_bytes=60 << 20
        ),
    )(cost_first, cost_second, factors, slab_factors, weights.reshape(1, RANK))
    new, marginal = pl.pallas_call(
        finish,
        out_shape=shapes,
        in_specs=[vmem] * 2,
        out_specs=(hbm, hbm),
        scratch_shapes=[dma((2,))],
        compiler_params=pltpu.CompilerParams(vmem_limit_bytes=1 << 20),
    )(new, marginal)
    return new, marginal.reshape(RANK)


def solution(mesh):
    placed = (P("row", "col"), P("row", "col"), P(("col", "row"), None), P("row", None), P())
    return jax.shard_map(
        local, mesh=mesh, in_specs=placed, out_specs=(P("row", None), P()), check_vma=False
    )
```

```python
import math

import jax
import jax.numpy as jnp
from jax import lax
from jax.experimental import pallas as pl
from jax.experimental.pallas import tpu as pltpu
from jax.sharding import PartitionSpec as P

MESH = pl.DeviceIdType.MESH
HIGH = lax.Precision.HIGHEST

NX, NY, NZ = 4, 4, 8
RANK = 64
LANES = 2 * RANK
ROWS = 128
DEEP = 400
BLOCKS = 64
SLOT = 512
N = 102400
SLAB = 8192

AHEAD = 9
LINKS = ((1, 0), (-1, 0), (0, 1), (0, -1))
CHUNKS = ((0, 112), (112, 96), (208, 96), (304, 96))
SENT = (
    (
        65, 67, 66, 64, 122, 123, 72, 120, 75, 128, 137, 80, 136, 82, 138, 83,
        112, 144, 139, 89, 90, 107, 91, 177, 186, 99, 42, 98, 97, 131, 130,
    ),
    (
        193, 194, 192, 195, 250, 200, 248, 203, 129, 201, 242, 243, 208, 210, 209, 240,
        241, 178, 179, 217, 146, 147, 176, 170, 218, 187, 224, 225, 168, 169, 163,
    ),
    (
        8, 10, 9, 11, 73, 16, 17, 18, 74, 19, 202, 81, 24, 25, 26, 211,
        27, 145, 88, 32, 33, 34, 216, 153, 152, 96, 154, 155, 219, 161, 160,
    ),
    (
        58, 59, 56, 57, 50, 51, 249, 121, 251, 48, 49, 114, 43, 115, 113, 185,
        184, 234, 235, 35, 40, 41, 232, 233, 227, 171, 104, 226, 105, 106, 162,
    ),
)
TURNS = (
    65, 193, 58, 8, 67, 194, 59, 10, 66, 192, 9, 56, 64, 195, 11, 57,
    -1, -9, -25, -2, -8, 73, 122, 250, 50, 16, 123, 51, 200, 17, 72, 249,
    248, 18, 121, 120, 203, 74, 251, 75, -16, 129, -32, 19, 48, 128, 201, 202,
    49, 137, 242, 81, 114, -10, 80, 243, 24, 43, 136, 208, -3, 25, 115, 82,
    210, 26, 113, 138, 209, -26, 211, 185, -7, 83, 240, 27, 184, -27, 112, 241,
    145, 234, 178, 144, 88, 235, -11, 179, 139, 35, 32, 217, 89, -4, 33, 40,
    146, 90, -15, 34, 41, 147, 107, -31, 216, 232, 176, 91, -18, 153, 233, 170,
    177, -5, -19, 152, 227, 218, 186, -12, -30, 171, 96, 187, 99, -23, -24, 104,
    42, 224, 154, -6, 226, 98, 225, 155, -29, -20, 105, 97, 219, 168, -13, -28,
    106, 131, 161, 169, -14, -22, 162, 130, -17, 163, 160, -21,
)


def kernel(
    cost_first, cost_second, factors, slab_in, weights_in, new, marginal,
    slab, twin_slab, weights, costs, twins, slots, total, turned, halves, outgoing, prods,
    stat, scattered, crossed, gathered, sums,
    load_sem, own_sem, send_sem, ring_sem, twin_sem, slab_sem, half_sem,
    small_send, scatter_sem, cross_sem, gather_sem, prod_sem, sum_sem,
):
    row = lax.axis_index("row")
    y = lax.axis_index("col")
    core = lax.rem(row, 2)
    z = lax.rem(row // 2, NZ)
    x = row // (2 * NZ)
    sign = 1 - 2 * core

    def device(dx, dy, dz, dc):
        xx = lax.rem(x + dx + NX, NX)
        yy = lax.rem(y + dy + NY, NY)
        zz = lax.rem(z + dz + NZ, NZ)
        cc = lax.rem(core + dc, 2)
        return ((xx * NZ + zz) * 2 + cc, yy)

    def signed(step, ring):
        return step - ring if step > ring // 2 else step

    where_x, where_z, shift_z = {}, {}, {}
    for away in (False, True):
        way, c = (-sign, 1 - core) if away else (sign, core)
        for dx in range(NX):
            where_x[away, dx] = lax.rem(x - way * signed(dx, NX) + NX, NX) * NZ
        for dz in range(NZ):
            where_z[away, dz] = lax.rem(z - way * signed(dz, NZ) + NZ, NZ)
            shift_z[away, dz] = 16 * lax.rem(2 * where_z[away, dz] + c, 8)

    def home(offset, away=False):
        return where_x[away, offset[0]] + where_z[away, offset[1]]

    def span(offset, start, size):
        return pl.ds(pl.multiple_of(shift_z[False, offset[1]] + start, 16), size)

    def column(offset, away):
        c = 1 - core if away else core
        first = 2 * DEEP * home(offset, away) + DEEP * c - shift_z[away, offset[1]]
        return pl.ds(pl.multiple_of(first, 128), SLOT)

    def remote(src, dst, send, recv, to):
        return pltpu.make_async_remote_copy(
            src_ref=src, dst_ref=dst, send_sem=send, recv_sem=recv,
            device_id=to, device_id_type=MESH,
        )

    load_first = pltpu.make_async_copy(cost_first, costs.at[pl.ds(0, ROWS)], load_sem.at[0])
    load_second = pltpu.make_async_copy(cost_second, costs.at[pl.ds(ROWS, ROWS)], load_sem.at[1])
    place = x * NZ + z
    own_slot = slots.at[place, span((0, 0), 0, DEEP)]
    load_own = pltpu.make_async_copy(factors, own_slot, own_sem)
    load_slab = pltpu.make_async_copy(slab_in, slab, load_sem.at[2])
    load_weights = pltpu.make_async_copy(weights_in, weights, load_sem.at[3])

    barrier = pltpu.get_barrier_semaphore()
    pairs = [(dy, dc) for dy in (2, 1, 3, 0) for dc in (1, 0) if (dy, dc) != (0, 0)]
    greeted = [device(ux, 0, uz, 0) for ux, uz in LINKS]
    greeted += [device(0, dy, 0, dc) for dy, dc in pairs]
    for to in greeted:
        pl.semaphore_signal(barrier, inc=1, device_id=to, device_id_type=MESH)
    load_slab.start()
    load_weights.start()
    load_own.start()
    load_first.start()
    load_second.start()
    pl.semaphore_wait(barrier, len(greeted))

    neighbour = [device(sign * ux, 0, sign * uz, 0) for ux, uz in LINKS]
    twin = device(0, 0, 0, 1)
    heads = [0] * len(LINKS)
    here = {chunk for chunk in range(len(CHUNKS))}

    def spot(offset, chunk):
        start, size = CHUNKS[chunk]
        return slots.at[home(offset), span(offset, start, size)]

    def send_ready():
        progress = True
        while progress:
            progress = False
            for link, (ux, uz) in enumerate(LINKS):
                if heads[link] < len(SENT[link]):
                    code = SENT[link][heads[link]]
                    dx, dz, chunk = code // 64, code // 8 % 8, code % 8
                    dx, dz = (dx - ux) % NX, (dz - uz) % NZ
                    if 64 * dx + 8 * dz + chunk in here:
                        dst = spot((dx, dz), chunk)
                        src = factors.at[pl.ds(*CHUNKS[chunk])] if dx == dz == 0 else dst
                        remote(
                            src, dst, send_sem.at[0], ring_sem.at[code], neighbour[link]
                        ).start()
                        heads[link] += 1
                        progress = True

    send_ready()

    order = [((-1 - turn) // 8, (-1 - turn) % 8) for turn in TURNS if turn < 0]

    def lend(indices):
        for k in indices:
            if k < len(order):
                at = column(order[k], True)
                for part, cost in enumerate((cost_first, cost_second)):
                    remote(
                        cost.at[:, at], twins.at[k, pl.ds(part * ROWS, ROWS)],
                        send_sem.at[1], twin_sem.at[k], twin,
                    ).start()

    lend(range(AHEAD))
    remote(slab_in, twin_slab, send_sem.at[2], slab_sem, twin).start()

    blank = jnp.zeros((16, LANES), jnp.bfloat16)

    def clear(group, carry):
        for j in range(4):
            m = 2 * j + core
            for i in range(7):
                at = pl.multiple_of(16 * (i + jnp.where(i < m, 0, DEEP // 16)), 16)
                slots[group * 4 + j, pl.ds(at, 16), :] = blank
        return carry

    lax.fori_loop(0, NX * NZ // 4, clear, 0)
    total[...] = jnp.zeros_like(total)

    def multiply(k):
        lend(range(k + AHEAD, k + AHEAD + 1))
        if k == 0:
            load_own.wait()
            load_first.wait()
            load_second.wait()
        ref = twins.at[k]
        pltpu.make_async_copy(ref, ref, twin_sem.at[k]).wait()
        left = jnp.concatenate([costs[:, column(order[k], False)], ref[...]], axis=0)
        total[...] += jnp.dot(left, slots[home(order[k])], preferred_element_type=jnp.float32)

    def split():
        load_slab.wait()
        load_weights.wait()
        remote(slab_in, twin_slab, send_sem.at[2], slab_sem, twin).wait_recv()
        rest = jnp.concatenate([slab[...].T, twin_slab[...].T], axis=1)
        for part in range(3):
            turned[pl.ds(part * LANES, LANES), :] = rest.astype(jnp.bfloat16)
            rest = rest - rest.astype(jnp.bfloat16).astype(jnp.float32)

    done = 0
    for turn in TURNS:
        if turn < 0:
            multiply(done)
            done += 1
            if done == 12:
                split()
        else:
            chunk = spot((turn // 64, turn // 8 % 8), turn % 8)
            remote(chunk, chunk, send_sem.at[0], ring_sem.at[turn], neighbour[0]).wait_recv()
            here.add(turn)
            send_ready()

    half = lax.broadcasted_iota(jnp.int32, (1, LANES), 1) < RANK
    scale = 1.0 / (16.0 * math.sqrt(N))
    part = jnp.where(half, total[0:ROWS, :], total[ROWS : 2 * ROWS, :]) * scale
    lent = jnp.where(half, total[2 * ROWS : 3 * ROWS, :], total[3 * ROWS :, :]) * scale
    rest = jnp.concatenate([part, lent], axis=0)
    pairs_of = []
    for count in (3, 2, 1):
        piece = rest.astype(jnp.bfloat16)
        rest = rest - piece.astype(jnp.float32)
        pairs_of.append(
            jnp.dot(
                turned[0 : count * LANES, :], piece, preferred_element_type=jnp.float32
            )
        )
    one, two, three = pairs_of
    small = one[2 * LANES :] + two[LANES:] + three
    terms = one[0:LANES] + ((one[LANES : 2 * LANES] + two[0:LANES]) + small)
    stat[...] = jnp.where(half, terms[0:RANK, :], terms[RANK:, :])

    me = y * 2 + core
    scattered[me] = stat[pl.ds(pl.multiple_of(8 * me, 8), 8), :]
    for dy, dc in pairs:
        to = device(0, dy, 0, dc)
        g = to[1] * 2 + lax.rem(to[0], 2)
        remote(
            stat.at[pl.ds(pl.multiple_of(8 * g, 8), 8)], scattered.at[me],
            small_send.at[0], scatter_sem.at[0], to,
        ).start()
    outgoing[...] = lent
    hand = remote(outgoing, halves.at[core], small_send.at[5], half_sem, twin)
    hand.start()
    halves[core] = part
    seven = scattered.at[pl.ds(0, len(pairs))]
    pltpu.make_async_copy(seven, seven, scatter_sem.at[0]).wait()
    piece = scattered[0]
    for g in range(1, 8):
        piece = piece + scattered[g]
    crossed[place] = piece
    far = [
        (dx, dz) for dz in (4, 3, 5, 2, 6, 1, 7, 0) for dx in (2, 1, 3, 0) if (dx, dz) != (0, 0)
    ]
    for dx, dz in far:
        remote(
            crossed.at[place], crossed.at[place], small_send.at[1], cross_sem.at[0],
            device(dx, 0, dz, 0),
        ).start()
    hand.wait()
    prods[y] = halves[0] + halves[1]
    for dy in (2, 1, 3):
        remote(
            prods.at[y], prods.at[y], small_send.at[2], prod_sem.at[0], device(0, dy, 0, 0)
        ).start()
    others = crossed.at[pl.ds(0, len(far))]
    pltpu.make_async_copy(others, others, cross_sem.at[0]).wait()
    piece = jnp.sum(crossed[...], axis=0)
    mine_rows = pl.ds(pl.multiple_of(8 * me, 8), 8)
    gathered[mine_rows, :] = piece
    for dy, dc in pairs:
        remote(
            gathered.at[mine_rows], gathered.at[mine_rows], small_send.at[3], gather_sem.at[0],
            device(0, dy, 0, dc),
        ).start()
    three = prods.at[pl.ds(0, NY - 1)]
    pltpu.make_async_copy(three, three, prod_sem.at[0]).wait()
    inverse = 1.0 / weights[...]
    inverse = jnp.concatenate([inverse, inverse], axis=1)
    product = ((prods[0] + prods[1]) + prods[2]) + prods[3]
    product = product * inverse
    most = gathered.at[pl.ds(0, 8 * len(pairs))]
    pltpu.make_async_copy(most, most, gather_sem.at[0]).wait()
    stats = gathered[...] * (1.0 / math.sqrt(SLAB))
    swapped = jnp.concatenate([stats[:, RANK:], stats[:, :RANK]], axis=1) * inverse
    both = jnp.concatenate(
        [jnp.where(half, swapped, 0.0), jnp.where(half, 0.0, swapped)], axis=0
    )
    move = jnp.dot(product, both, precision=HIGH, preferred_element_type=jnp.float32)
    move = move * (1.0 / math.sqrt(RANK))
    low = jnp.max(jnp.where(half, move, -jnp.inf), axis=1, keepdims=True)
    high = jnp.max(jnp.where(half, -jnp.inf, move), axis=1, keepdims=True)
    tilde = slab[...] * jnp.exp(move - jnp.where(half, low, high))
    low = jnp.sum(jnp.where(half, tilde, 0.0), axis=1, keepdims=True)
    high = jnp.sum(jnp.where(half, 0.0, tilde), axis=1, keepdims=True)
    result = tilde / jnp.where(half, low, high)
    sums[row] = jnp.sum(result, axis=0, keepdims=True)
    for dx, dz in far + [(0, 0)]:
        for dc in (0, 1):
            if (dx, dz, dc) != (0, 0, 0):
                remote(
                    sums.at[row], sums.at[row], small_send.at[4], sum_sem.at[0],
                    device(dx, 0, dz, dc),
                ).start()
    new[...] = result

    rest = sums.at[pl.ds(0, BLOCKS - 1)]
    sent = slots.at[pl.ds(0, NX * NZ - 1), pl.ds(0, DEEP)]
    pltpu.make_async_copy(sent, sent, send_sem.at[0]).wait()
    pltpu.make_async_copy(twins, twins, send_sem.at[1]).wait()
    remote(slab_in, twin_slab, send_sem.at[2], slab_sem, twin).wait_send()
    pltpu.make_async_copy(seven, seven, small_send.at[0]).wait()
    pltpu.make_async_copy(others, others, small_send.at[1]).wait()
    pltpu.make_async_copy(three, three, small_send.at[2]).wait()
    pltpu.make_async_copy(most, most, small_send.at[3]).wait()
    pltpu.make_async_copy(rest, rest, sum_sem.at[0]).wait()
    sums_all = jnp.sum(sums[...], axis=0)
    marginal[...] = (RANK / (2.0 * SLAB)) * (sums_all[:, :RANK] + sums_all[:, RANK:])
    pltpu.make_async_copy(rest, rest, small_send.at[4]).wait()


def finish(new_in, marginal_in, new, marginal, sems):
    first = pltpu.make_async_copy(new_in, new, sems.at[0])
    second = pltpu.make_async_copy(marginal_in, marginal, sems.at[1])
    first.start()
    second.start()
    first.wait()
    second.wait()


def local(cost_first, cost_second, factors, slab_factors, weights):
    hbm = pl.BlockSpec(memory_space=pltpu.HBM)
    vmem = pl.BlockSpec(memory_space=pltpu.VMEM)
    f32, bf16 = jnp.float32, jnp.bfloat16
    dma = pltpu.SemaphoreType.DMA
    shapes = (
        jax.ShapeDtypeStruct((ROWS, LANES), f32),
        jax.ShapeDtypeStruct((1, RANK), f32),
    )
    new, marginal = pl.pallas_call(
        kernel,
        out_shape=tuple(pltpu.VMEM(shape.shape, shape.dtype) for shape in shapes),
        in_specs=[hbm] * 5,
        out_specs=(vmem, vmem),
        scratch_shapes=[
            pltpu.VMEM((ROWS, LANES), f32),
            pltpu.VMEM((ROWS, LANES), f32),
            pltpu.VMEM((1, RANK), f32),
            pltpu.VMEM((2 * ROWS, BLOCKS * DEEP), bf16),
            pltpu.VMEM((NX * NZ, 2 * ROWS, SLOT), bf16),
            pltpu.VMEM((NX * NZ, SLOT, LANES), bf16),
            pltpu.VMEM((4 * ROWS, LANES), f32),
            pltpu.VMEM((3 * LANES, 2 * ROWS), bf16),
            pltpu.VMEM((2, ROWS, LANES), f32),
            pltpu.VMEM((ROWS, LANES), f32),
            pltpu.VMEM((NY, ROWS, LANES), f32),
            pltpu.VMEM((RANK, LANES), f32),
            pltpu.VMEM((8, 8, LANES), f32),
            pltpu.VMEM((NX * NZ, 8, LANES), f32),
            pltpu.VMEM((RANK, LANES), f32),
            pltpu.VMEM((BLOCKS, 1, LANES), f32),
            dma((4,)),
            dma,
            dma((3,)),
            dma((8 * NX * NZ,)),
            dma((NX * NZ,)),
            dma,
            dma,
            dma((6,)),
            dma((1,)),
            dma((1,)),
            dma((1,)),
            dma((1,)),
            dma((1,)),
        ],
        compiler_params=pltpu.CompilerParams(
            collective_id=0, has_side_effects=True, vmem_limit_bytes=60 << 20
        ),
    )(cost_first, cost_second, factors, slab_factors, weights.reshape(1, RANK))
    new, marginal = pl.pallas_call(
        finish,
        out_shape=shapes,
        in_specs=[vmem] * 2,
        out_specs=(hbm, hbm),
        scratch_shapes=[dma((2,))],
        compiler_params=pltpu.CompilerParams(vmem_limit_bytes=1 << 20),
    )(new, marginal)
    return new, marginal.reshape(RANK)


def solution(mesh):
    placed = (P("row", "col"), P("row", "col"), P(("col", "row"), None), P("row", None), P())
    return jax.shard_map(
        local, mesh=mesh, in_specs=placed, out_specs=(P("row", None), P()), check_vma=False
    )
```

```python
import math

import jax
import jax.numpy as jnp
from jax import lax
from jax.experimental import pallas as pl
from jax.experimental.pallas import tpu as pltpu
from jax.sharding import PartitionSpec as P

MESH = pl.DeviceIdType.MESH
HIGH = lax.Precision.HIGHEST

NX, NY, NZ = 4, 4, 8
RANK = 64
LANES = 2 * RANK
ROWS = 128
DEEP = 400
BLOCKS = 64
SLOT = 512
N = 102400
SLAB = 8192

AHEAD = 9
LINKS = ((1, 0), (-1, 0), (0, 1), (0, -1))
CHUNKS = ((0, 112), (112, 96), (208, 96), (304, 96))
SENT = (
    (
        67, 66, 64, 65, 131, 130, 72, 120, 128, 121, 139, 80, 136, 184, 138, 113,
        186, 144, 106, 147, 90, 89, 107, 81, 98, 170, 155, 154, 153, 163, 162,
    ),
    (
        193, 194, 195, 192, 129, 200, 248, 203, 202, 250, 185, 242, 201, 243, 241, 210,
        209, 211, 123, 137, 216, 235, 234, 232, 219, 226, 233, 145, 171, 218, 225,
    ),
    (
        8, 11, 10, 9, 75, 16, 74, 18, 73, 17, 19, 83, 208, 24, 26, 25,
        27, 91, 88, 82, 32, 146, 33, 99, 152, 114, 96, 224, 217, 97, 160,
    ),
    (
        58, 56, 59, 57, 249, 50, 251, 51, 49, 48, 122, 187, 42, 240, 43, 112,
        40, 177, 34, 41, 35, 176, 104, 169, 105, 115, 179, 178, 168, 227, 161,
    ),
)
TURNS = (
    67, 193, 58, 8, 66, 194, 11, 56, -1, 195, 64, 10, 59, 65, 192, 9,
    57, -9, -25, -2, -8, 131, 75, 129, 249, 130, 16, 50, 200, 72, 74, 251,
    248, 18, 120, 51, 203, 73, 49, 128, 202, -10, 17, 121, 48, 250, -17, 19,
    122, 139, 185, -7, 83, 187, 80, 242, 208, 42, 201, 136, -32, 24, 240, 243,
    184, -3, 26, 43, 241, 138, -26, 25, 112, 210, 113, -31, 27, 40, 209, 186,
    -4, 91, 177, 211, 144, -24, 88, 34, 123, 106, 82, 41, 137, 147, -27, -16,
    32, 35, 216, 90, -6, 146, 235, 89, 176, 33, 234, 107, 104, -18, -12, 99,
    81, 232, 169, -5, -11, 152, 98, 219, 105, -14, 114, 170, 226, 115, -15, 155,
    233, 96, 179, -30, 154, 145, 178, 224, -19, -23, 153, 171, 217, 168, -20, -22,
    218, 163, 97, 227, -28, -13, 225, -29, 161, 160, 162, -21,
)


def kernel(
    cost_first, cost_second, factors, slab_in, weights_in, new, marginal,
    slab, twin_slab, weights, costs, twins, slots, total, turned, halves, outgoing, prods,
    stat, scattered, crossed, gathered, sums,
    load_sem, own_sem, send_sem, ring_sem, twin_sem, slab_sem, half_sem,
    small_send, scatter_sem, cross_sem, gather_sem, prod_sem, sum_sem,
):
    row = lax.axis_index("row")
    y = lax.axis_index("col")
    core = lax.rem(row, 2)
    z = lax.rem(row // 2, NZ)
    x = row // (2 * NZ)
    sign = 1 - 2 * core

    def device(dx, dy, dz, dc):
        xx = lax.rem(x + dx + NX, NX)
        yy = lax.rem(y + dy + NY, NY)
        zz = lax.rem(z + dz + NZ, NZ)
        cc = lax.rem(core + dc, 2)
        return ((xx * NZ + zz) * 2 + cc, yy)

    def signed(step, ring):
        return step - ring if step > ring // 2 else step

    where_x, where_z, shift_z = {}, {}, {}
    for away in (False, True):
        way, c = (-sign, 1 - core) if away else (sign, core)
        for dx in range(NX):
            where_x[away, dx] = lax.rem(x - way * signed(dx, NX) + NX, NX) * NZ
        for dz in range(NZ):
            where_z[away, dz] = lax.rem(z - way * signed(dz, NZ) + NZ, NZ)
            shift_z[away, dz] = 16 * lax.rem(2 * where_z[away, dz] + c, 8)

    def home(offset, away=False):
        return where_x[away, offset[0]] + where_z[away, offset[1]]

    def span(offset, start, size):
        return pl.ds(pl.multiple_of(shift_z[False, offset[1]] + start, 16), size)

    def column(offset, away):
        c = 1 - core if away else core
        first = 2 * DEEP * home(offset, away) + DEEP * c - shift_z[away, offset[1]]
        return pl.ds(pl.multiple_of(first, 128), SLOT)

    def remote(src, dst, send, recv, to):
        return pltpu.make_async_remote_copy(
            src_ref=src, dst_ref=dst, send_sem=send, recv_sem=recv,
            device_id=to, device_id_type=MESH,
        )

    load_first = pltpu.make_async_copy(cost_first, costs.at[pl.ds(0, ROWS)], load_sem.at[0])
    load_second = pltpu.make_async_copy(cost_second, costs.at[pl.ds(ROWS, ROWS)], load_sem.at[1])
    place = x * NZ + z
    own_slot = slots.at[place, span((0, 0), 0, DEEP)]
    load_own = pltpu.make_async_copy(factors, own_slot, own_sem)
    load_slab = pltpu.make_async_copy(slab_in, slab, load_sem.at[2])
    load_weights = pltpu.make_async_copy(weights_in, weights, load_sem.at[3])

    barrier = pltpu.get_barrier_semaphore()
    pairs = [(dy, dc) for dy in (2, 1, 3, 0) for dc in (1, 0) if (dy, dc) != (0, 0)]
    greeted = [device(ux, 0, uz, 0) for ux, uz in LINKS]
    greeted += [device(0, dy, 0, dc) for dy, dc in pairs]
    for to in greeted:
        pl.semaphore_signal(barrier, inc=1, device_id=to, device_id_type=MESH)
    load_slab.start()
    load_weights.start()
    load_own.start()
    load_first.start()
    load_second.start()
    pl.semaphore_wait(barrier, len(greeted))

    neighbour = [device(sign * ux, 0, sign * uz, 0) for ux, uz in LINKS]
    twin = device(0, 0, 0, 1)
    heads = [0] * len(LINKS)
    here = {chunk for chunk in range(len(CHUNKS))}

    def spot(offset, chunk):
        start, size = CHUNKS[chunk]
        return slots.at[home(offset), span(offset, start, size)]

    def send_ready():
        progress = True
        while progress:
            progress = False
            for link, (ux, uz) in enumerate(LINKS):
                if heads[link] < len(SENT[link]):
                    code = SENT[link][heads[link]]
                    dx, dz, chunk = code // 64, code // 8 % 8, code % 8
                    dx, dz = (dx - ux) % NX, (dz - uz) % NZ
                    if 64 * dx + 8 * dz + chunk in here:
                        dst = spot((dx, dz), chunk)
                        src = factors.at[pl.ds(*CHUNKS[chunk])] if dx == dz == 0 else dst
                        remote(
                            src, dst, send_sem.at[0], ring_sem.at[code], neighbour[link]
                        ).start()
                        heads[link] += 1
                        progress = True

    send_ready()

    order = [((-1 - turn) // 8, (-1 - turn) % 8) for turn in TURNS if turn < 0]

    def lend(indices):
        for k in indices:
            if k < len(order):
                at = column(order[k], True)
                for part, cost in enumerate((cost_first, cost_second)):
                    remote(
                        cost.at[:, at], twins.at[k, pl.ds(part * ROWS, ROWS)],
                        send_sem.at[1], twin_sem.at[k], twin,
                    ).start()

    lend(range(AHEAD))
    remote(slab_in, twin_slab, send_sem.at[2], slab_sem, twin).start()

    blank = jnp.zeros((16, LANES), jnp.bfloat16)

    def clear(group, carry):
        for j in range(4):
            m = 2 * j + core
            for i in range(7):
                at = pl.multiple_of(16 * (i + jnp.where(i < m, 0, DEEP // 16)), 16)
                slots[group * 4 + j, pl.ds(at, 16), :] = blank
        return carry

    lax.fori_loop(0, NX * NZ // 4, clear, 0)
    total[...] = jnp.zeros_like(total)

    def multiply(k):
        lend(range(k + AHEAD, k + AHEAD + 1))
        if k == 0:
            load_own.wait()
            load_first.wait()
            load_second.wait()
        ref = twins.at[k]
        pltpu.make_async_copy(ref, ref, twin_sem.at[k]).wait()
        left = jnp.concatenate([costs[:, column(order[k], False)], ref[...]], axis=0)
        total[...] += jnp.dot(left, slots[home(order[k])], preferred_element_type=jnp.float32)

    def split():
        load_slab.wait()
        load_weights.wait()
        remote(slab_in, twin_slab, send_sem.at[2], slab_sem, twin).wait_recv()
        rest = jnp.concatenate([slab[...].T, twin_slab[...].T], axis=1)
        for part in range(3):
            turned[pl.ds(part * LANES, LANES), :] = rest.astype(jnp.bfloat16)
            rest = rest - rest.astype(jnp.bfloat16).astype(jnp.float32)

    done = 0
    for turn in TURNS:
        if turn < 0:
            multiply(done)
            done += 1
            if done == 12:
                split()
        else:
            chunk = spot((turn // 64, turn // 8 % 8), turn % 8)
            remote(chunk, chunk, send_sem.at[0], ring_sem.at[turn], neighbour[0]).wait_recv()
            here.add(turn)
            send_ready()

    half = lax.broadcasted_iota(jnp.int32, (1, LANES), 1) < RANK
    scale = 1.0 / (16.0 * math.sqrt(N))
    part = jnp.where(half, total[0:ROWS, :], total[ROWS : 2 * ROWS, :]) * scale
    lent = jnp.where(half, total[2 * ROWS : 3 * ROWS, :], total[3 * ROWS :, :]) * scale
    rest = jnp.concatenate([part, lent], axis=0)
    pairs_of = []
    for count in (3, 2, 1):
        piece = rest.astype(jnp.bfloat16)
        rest = rest - piece.astype(jnp.float32)
        pairs_of.append(
            jnp.dot(
                turned[0 : count * LANES, :], piece, preferred_element_type=jnp.float32
            )
        )
    one, two, three = pairs_of
    small = one[2 * LANES :] + two[LANES:] + three
    terms = one[0:LANES] + ((one[LANES : 2 * LANES] + two[0:LANES]) + small)
    stat[...] = jnp.where(half, terms[0:RANK, :], terms[RANK:, :])

    me = y * 2 + core
    scattered[me] = stat[pl.ds(pl.multiple_of(8 * me, 8), 8), :]
    for dy, dc in pairs:
        to = device(0, dy, 0, dc)
        g = to[1] * 2 + lax.rem(to[0], 2)
        remote(
            stat.at[pl.ds(pl.multiple_of(8 * g, 8), 8)], scattered.at[me],
            small_send.at[0], scatter_sem.at[0], to,
        ).start()
    outgoing[...] = lent
    hand = remote(outgoing, halves.at[core], small_send.at[5], half_sem, twin)
    hand.start()
    halves[core] = part
    seven = scattered.at[pl.ds(0, len(pairs))]
    pltpu.make_async_copy(seven, seven, scatter_sem.at[0]).wait()
    piece = scattered[0]
    for g in range(1, 8):
        piece = piece + scattered[g]
    crossed[place] = piece

    def farthest_first(send):
        def one(i, carry):
            dz = NZ // 2 + (i + 1) // 2 * (1 - 2 * lax.rem(i, 2))
            for dx in (2, 1, 3, 0):
                send(dx, dz)
            return carry

        lax.fori_loop(0, NZ - 1, one, 0)
        for dx in (2, 1, 3):
            send(dx, 0)

    def send_piece(dx, dz):
        remote(
            crossed.at[place], crossed.at[place], small_send.at[1], cross_sem.at[0],
            device(dx, 0, dz, 0),
        ).start()

    farthest_first(send_piece)
    hand.wait()
    prods[y] = halves[0] + halves[1]
    for dy in (2, 1, 3):
        remote(
            prods.at[y], prods.at[y], small_send.at[2], prod_sem.at[0], device(0, dy, 0, 0)
        ).start()
    others = crossed.at[pl.ds(0, NX * NZ - 1)]
    pltpu.make_async_copy(others, others, cross_sem.at[0]).wait()
    piece = jnp.sum(crossed[...], axis=0)
    mine_rows = pl.ds(pl.multiple_of(8 * me, 8), 8)
    gathered[mine_rows, :] = piece
    for dy, dc in pairs:
        remote(
            gathered.at[mine_rows], gathered.at[mine_rows], small_send.at[3], gather_sem.at[0],
            device(0, dy, 0, dc),
        ).start()
    three = prods.at[pl.ds(0, NY - 1)]
    pltpu.make_async_copy(three, three, prod_sem.at[0]).wait()
    inverse = 1.0 / weights[...]
    inverse = jnp.concatenate([inverse, inverse], axis=1)
    product = ((prods[0] + prods[1]) + prods[2]) + prods[3]
    product = product * inverse
    most = gathered.at[pl.ds(0, 8 * len(pairs))]
    pltpu.make_async_copy(most, most, gather_sem.at[0]).wait()
    stats = gathered[...] * (1.0 / math.sqrt(SLAB))
    swapped = jnp.concatenate([stats[:, RANK:], stats[:, :RANK]], axis=1) * inverse
    both = jnp.concatenate(
        [jnp.where(half, swapped, 0.0), jnp.where(half, 0.0, swapped)], axis=0
    )
    move = jnp.dot(product, both, precision=HIGH, preferred_element_type=jnp.float32)
    move = move * (1.0 / math.sqrt(RANK))
    low = jnp.max(jnp.where(half, move, -jnp.inf), axis=1, keepdims=True)
    high = jnp.max(jnp.where(half, -jnp.inf, move), axis=1, keepdims=True)
    tilde = slab[...] * jnp.exp(move - jnp.where(half, low, high))
    low = jnp.sum(jnp.where(half, tilde, 0.0), axis=1, keepdims=True)
    high = jnp.sum(jnp.where(half, 0.0, tilde), axis=1, keepdims=True)
    result = tilde / jnp.where(half, low, high)
    sums[row] = jnp.sum(result, axis=0, keepdims=True)

    def send_sums(dx, dz):
        for dc in (0, 1):
            remote(
                sums.at[row], sums.at[row], small_send.at[4], sum_sem.at[0],
                device(dx, 0, dz, dc),
            ).start()

    farthest_first(send_sums)
    remote(sums.at[row], sums.at[row], small_send.at[4], sum_sem.at[0], twin).start()
    new[...] = result

    rest = sums.at[pl.ds(0, BLOCKS - 1)]
    sent = slots.at[pl.ds(0, NX * NZ - 1), pl.ds(0, DEEP)]
    pltpu.make_async_copy(sent, sent, send_sem.at[0]).wait()
    pltpu.make_async_copy(twins, twins, send_sem.at[1]).wait()
    remote(slab_in, twin_slab, send_sem.at[2], slab_sem, twin).wait_send()
    pltpu.make_async_copy(seven, seven, small_send.at[0]).wait()
    pltpu.make_async_copy(others, others, small_send.at[1]).wait()
    pltpu.make_async_copy(three, three, small_send.at[2]).wait()
    pltpu.make_async_copy(most, most, small_send.at[3]).wait()
    pltpu.make_async_copy(rest, rest, sum_sem.at[0]).wait()
    sums_all = jnp.sum(sums[...], axis=0)
    marginal[...] = (RANK / (2.0 * SLAB)) * (sums_all[:, :RANK] + sums_all[:, RANK:])
    pltpu.make_async_copy(rest, rest, small_send.at[4]).wait()


def finish(new_in, marginal_in, new, marginal, sems):
    first = pltpu.make_async_copy(new_in, new, sems.at[0])
    second = pltpu.make_async_copy(marginal_in, marginal, sems.at[1])
    first.start()
    second.start()
    first.wait()
    second.wait()


def local(cost_first, cost_second, factors, slab_factors, weights):
    hbm = pl.BlockSpec(memory_space=pltpu.HBM)
    vmem = pl.BlockSpec(memory_space=pltpu.VMEM)
    f32, bf16 = jnp.float32, jnp.bfloat16
    dma = pltpu.SemaphoreType.DMA
    shapes = (
        jax.ShapeDtypeStruct((ROWS, LANES), f32),
        jax.ShapeDtypeStruct((1, RANK), f32),
    )
    new, marginal = pl.pallas_call(
        kernel,
        out_shape=tuple(pltpu.VMEM(shape.shape, shape.dtype) for shape in shapes),
        in_specs=[hbm] * 5,
        out_specs=(vmem, vmem),
        scratch_shapes=[
            pltpu.VMEM((ROWS, LANES), f32),
            pltpu.VMEM((ROWS, LANES), f32),
            pltpu.VMEM((1, RANK), f32),
            pltpu.VMEM((2 * ROWS, BLOCKS * DEEP), bf16),
            pltpu.VMEM((NX * NZ, 2 * ROWS, SLOT), bf16),
            pltpu.VMEM((NX * NZ, SLOT, LANES), bf16),
            pltpu.VMEM((4 * ROWS, LANES), f32),
            pltpu.VMEM((3 * LANES, 2 * ROWS), bf16),
            pltpu.VMEM((2, ROWS, LANES), f32),
            pltpu.VMEM((ROWS, LANES), f32),
            pltpu.VMEM((NY, ROWS, LANES), f32),
            pltpu.VMEM((RANK, LANES), f32),
            pltpu.VMEM((8, 8, LANES), f32),
            pltpu.VMEM((NX * NZ, 8, LANES), f32),
            pltpu.VMEM((RANK, LANES), f32),
            pltpu.VMEM((BLOCKS, 1, LANES), f32),
            dma((4,)),
            dma,
            dma((3,)),
            dma((8 * NX * NZ,)),
            dma((NX * NZ,)),
            dma,
            dma,
            dma((6,)),
            dma((1,)),
            dma((1,)),
            dma((1,)),
            dma((1,)),
            dma((1,)),
        ],
        compiler_params=pltpu.CompilerParams(
            collective_id=0, has_side_effects=True, vmem_limit_bytes=60 << 20
        ),
    )(cost_first, cost_second, factors, slab_factors, weights.reshape(1, RANK))
    new, marginal = pl.pallas_call(
        finish,
        out_shape=shapes,
        in_specs=[vmem] * 2,
        out_specs=(hbm, hbm),
        scratch_shapes=[dma((2,))],
        compiler_params=pltpu.CompilerParams(vmem_limit_bytes=1 << 20),
    )(new, marginal)
    return new, marginal.reshape(RANK)


def solution(mesh):
    placed = (P("row", "col"), P("row", "col"), P(("col", "row"), None), P("row", None), P())
    return jax.shard_map(
        local, mesh=mesh, in_specs=placed, out_specs=(P("row", None), P()), check_vma=False
    )
```
